512 devices in a mesh: dp: 512 (over y, z, x, core).
Axes of the slice: x: 4, y: 8, z: 8, core: 2. Of those that a mesh axis runs over, the one named last changes fastest.
Arguments:
- entry_input: bfloat16 [65536, 3072], P('dp'), may hold values from -6 to 6
- entry_grad: bfloat16 [65536, 6144], P('dp'), may hold values from -6 to 6
- exit_input: bfloat16 [65536, 4096], P('dp'), may hold values from -6 to 6
- exit_grad: bfloat16 [65536, 3072], P('dp'), may hold values from -6 to 6
- entry_left: bfloat16 [8192, 3072], P('dp'), may hold values from -6 to 6
- entry_right: bfloat16 [8192, 6144], P('dp'), may hold values from -6 to 6
- exit_left: bfloat16 [8192, 4096], P('dp'), may hold values from -6 to 6
- exit_right: bfloat16 [8192, 3072], P('dp'), may hold values from -6 to 6
- entry_start: float32 [6144, 32], P('dp'), may hold values from -6 to 6
- exit_start: float32 [3072, 32], P('dp'), may hold values from -6 to 6
Outputs:
- entry_basis: float32 [3072, 32], P('dp')
- exit_basis: float32 [4096, 32], P('dp')
- entry_factor: float32 [6144, 32], P('dp')
- exit_factor: float32 [3072, 32], P('dp')
The draws below stay inside these ranges and needn't reach their ends.
All inputs are finite; a program needn't handle non-finite values.
Results may differ from the reference program's by a relative error of at most 0.0003.
Values sent between devices are 32-bit elements; how exact they have to be, the bound alone decides.
A program may use at most 64 MiB of HBM per device.

```python
import math
import jax
import jax.numpy as jnp
from jax import lax

D = 3072
QKV = 6144
ATTN = 4096
RANK = 32
TOKENS = 65536
RESID = 8192
N_DP = 512


def block_levels(rng, shape, split, least, top_value):
    loudness = 1.0
    for axis_at, blocks in split:
        heights = jax.random.uniform(jax.random.fold_in(jax.random.fold_in(rng, 6), axis_at), (blocks,), jnp.float32, least / len(split), top_value / len(split))
        loudness = loudness * jnp.repeat(jnp.exp(heights), shape[axis_at] // blocks).reshape((-1,) + (1,) * (len(shape) - 1 - axis_at))
    return loudness


def bell_draw(own_key, dims, scale, most, split=(), held_as=jnp.bfloat16):
    gain = block_levels(own_key, dims, split, -0.22, 0.18) if split else 1.0
    values = jax.random.normal(own_key, dims, jnp.float32) * scale * gain
    return jnp.minimum(jnp.maximum(values, -most), most).astype(held_as)


def setup_inputs(seed: int = 0) -> dict:
    arg_keys = jax.random.split(jax.random.key(seed), 11)
    return {
        "entry_input": bell_draw(arg_keys[0], (TOKENS, D), 1.0, 6.0, ((0, 512),)),
        "entry_grad": bell_draw(arg_keys[1], (TOKENS, QKV), 1.0, 6.0, ((0, 512),)),
        "exit_input": bell_draw(arg_keys[2], (TOKENS, ATTN), 1.0, 6.0, ((0, 512),)),
        "exit_grad": bell_draw(arg_keys[3], (TOKENS, D), 1.0, 6.0, ((0, 512),)),
        "entry_left": bell_draw(arg_keys[4], (RESID, D), 1.0, 6.0, ((0, 512),)),
        "entry_right": bell_draw(arg_keys[5], (RESID, QKV), 1.0, 6.0, ((0, 512),)),
        "exit_left": bell_draw(arg_keys[6], (RESID, ATTN), 1.0, 6.0, ((0, 512),)),
        "exit_right": bell_draw(arg_keys[7], (RESID, D), 1.0, 6.0, ((0, 512),)),
        "entry_start": bell_draw(arg_keys[8], (QKV, RANK), 1.0, 6.0, ((0, 512),), jnp.float32),
        "exit_start": bell_draw(arg_keys[9], (D, RANK), 1.0, 6.0, ((0, 512),), jnp.float32),
    }


def product(a, b):
    return jnp.dot(a.astype(jnp.float32), b.astype(jnp.float32), precision=lax.Precision.HIGHEST, preferred_element_type=jnp.float32)

def compress(inputs, grads, left_rows, right_rows, start, width):
    inputs = inputs.astype(jnp.float32)
    grads = grads.astype(jnp.float32)
    left_rows = left_rows.astype(jnp.float32)
    right_rows = right_rows.astype(jnp.float32)
    projected = product(grads, start)
    carried = product(right_rows, start)
    summed_left = product(inputs.T, projected) + product(left_rows.T, carried)
    gram = product(summed_left.T, summed_left)
    lower = jnp.linalg.cholesky(gram)
    basis = jax.scipy.linalg.solve_triangular(lower, summed_left.T, lower=True).T
    token_side = product(inputs, basis)
    resid_side = product(left_rows, basis)
    factor = (product(grads.T, token_side) + product(right_rows.T, resid_side)) / N_DP
    return (basis * math.sqrt(width), factor)

def reference(entry_input, entry_grad, exit_input, exit_grad, entry_left, entry_right, exit_left, exit_right, entry_start, exit_start):
    entry_basis, entry_factor = compress(entry_input, entry_grad, entry_left, entry_right, entry_start, D)
    exit_basis, exit_factor = compress(exit_input, exit_grad, exit_left, exit_right, exit_start, ATTN)
    return (entry_basis, exit_basis, entry_factor, exit_factor)
```

```python
import functools
import math

import jax
import jax.numpy as jnp
from jax import lax
from jax.experimental import pallas as pl
from jax.experimental.pallas import tpu as pltpu
from jax.sharding import PartitionSpec as P

MESH = pl.DeviceIdType.MESH
NY, NZ, NX = 8, 8, 4
GROUPS = 4
HALF = 4
TOK = 144
NS = 9
NL = 7
F32 = jnp.float32
BF16 = jnp.bfloat16
NT = (((1,), (1,)), ((), ()))
NN = (((1,), (0,)), ((), ()))
TN = (((0,), (0,)), ((), ()))


def device(y, z, x, c):
    return ((y * NZ + z) * NX + x) * 2 + c


def split3(v):
    hi = v.astype(BF16)
    rest = v - hi.astype(F32)
    mid = rest.astype(BF16)
    lo = (rest - mid.astype(F32)).astype(BF16)
    return jnp.concatenate([hi, mid, lo], axis=0)


def fold3(v):
    return v[0:32] + v[32:64] + v[64:96]


def exact_dot(a, b, dims):
    return lax.dot_general(a, b, dims, precision=lax.Precision.HIGHEST, preferred_element_type=F32)


def entry_window(z):
    return 3 * (z // 4) + (z % 4) // 2


def exit_window(z):
    return z // 4


def iota(shape, dim):
    return lax.broadcasted_iota(jnp.int32, shape, dim)


def kernel(
    entry_input, entry_grad, exit_input, exit_grad,
    entry_left, entry_right, exit_left, exit_right,
    entry_start, exit_start,
    out,
    wxe, wge, wxx, wgx, own_start,
    s_all, l_all,
    first_send, first_recv, zs_send, zs_recv,
    l_loc, l_core, l_x, l_ys, l_y, l_zs, l_z,
    f_loc, f_core, f_x, f_ys, f_y, f_zs, f_z, f_last, f_own,
    load_sem,
    first_ss, first_rs, zs_ss, zs_rs, lz_ss, lz_rs, fz_ss, fz_rs, last_ss, last_rs,
    sg_ys, sg_yr, sg_xs, sg_xr, sg_cs, sg_cr,
    lg_ys, lg_yr, lg_xs, lg_xr, lg_cs, lg_cr,
    lr_cs, lr_cr, lr_xs, lr_xr, lr_ys, lr_yr,
    fr_cs, fr_cr, fr_xs, fr_xr, fr_ys, fr_yr,
):
    me = lax.axis_index("dp")
    y, z, x, c = me // (NZ * NX * 2), (me // (NX * 2)) % NZ, (me // 2) % NX, me % 2
    active_core = y // HALF
    active = c == active_core
    other = device(y, z, x, 1 - c)
    spot = 2 * x + c
    pending = []

    def remote(src, dst, ss, rs, target):
        return pltpu.make_async_remote_copy(
            src_ref=src, dst_ref=dst, send_sem=ss, recv_sem=rs, device_id=(target,), device_id_type=MESH
        )

    def guarded(cond, fn):
        if cond is None:
            fn()
        else:
            @pl.when(cond)
            def _():
                fn()

    def send(src, dst, ss, rs, target, cond=None):
        copy = remote(src, dst, ss, rs, target)
        guarded(cond, copy.start)
        pending.append((cond, copy))

    def arrive(dst, ss, rs, cond=None):
        copy = remote(dst, dst, ss, rs, other)
        guarded(cond, copy.wait_recv)

    loads = []
    for i, (src, dst, row, rows) in enumerate((
        (entry_grad, wge, 0, 128), (entry_right, wge, 128, 16),
        (exit_grad, wgx, 0, 128), (exit_right, wgx, 128, 16),
        (entry_input, wxe, 0, 128), (entry_left, wxe, 128, 16),
        (exit_input, wxx, 0, 128), (exit_left, wxx, 128, 16),
    )):
        copy = pltpu.make_async_copy(src, dst.at[pl.ds(row, rows)], load_sem.at[i])
        copy.start()
        loads.append(copy)

    barrier = pltpu.get_barrier_semaphore()
    peers = [device(y, z, (x + k // 2) % NX, (c + k) % 2) for k in range(1, 8)]
    peers += [device(y, (z + k) % NZ, x, c) for k in range(1, 8)]
    peers += [device((y + k) % NY, z, x, c) for k in range(1, 8)]
    for peer in peers:
        pl.semaphore_signal(barrier, inc=1, device_id=(peer,), device_id_type=MESH)

    own_start[...] = jnp.zeros_like(own_start)
    own_start[0:12, :] = entry_start[...]
    own_start[16:22, :] = exit_start[...]
    at_entry = 96 * z - 128 * entry_window(z) + 12 * spot
    at_exit = 48 * z - 128 * exit_window(z) + 6 * spot
    pick_entry = jnp.where(
        (iota((16, 256), 1) == at_entry + iota((16, 256), 0)) & (iota((16, 256), 0) < 12), 1.0, 0.0
    ).astype(F32)
    pick_exit = jnp.where(
        (iota((16, 256), 1) == at_exit + iota((16, 256), 0)) & (iota((16, 256), 0) < 6), 1.0, 0.0
    ).astype(F32)
    placed_entry = exact_dot(own_start[0:16, :], pick_entry, TN)
    placed_exit = exact_dot(own_start[16:32, :], pick_exit, TN)
    for g in range(GROUPS):
        for t in range(2):
            first_send[g, t] = placed_entry[8 * g:8 * g + 8, 128 * t:128 * t + 128]
            first_send[g, 2 + t] = placed_exit[8 * g:8 * g + 8, 128 * t:128 * t + 128]

    pl.semaphore_wait(barrier, len(peers))

    send(first_send.at[x], first_recv.at[spot], first_ss.at[0], first_rs.at[spot], other, jnp.logical_not(active))
    for k in range(1, 4):
        to = (x + k) % NX
        send(first_send.at[to], first_recv.at[spot], first_ss.at[k], first_rs.at[spot], device(y, z, to, active_core))

    @pl.when(active)
    def _():
        total = [first_send[x, t] for t in range(4)]
        for k in range(1, 8):
            source = (spot + k) % 8
            arrive(first_recv.at[source], first_ss.at[0], first_rs.at[source])
            for t in range(4):
                total[t] = total[t] + first_recv[source, t]
        for t in range(4):
            zs_send[t] = total[t]

    for k in range(1, 8):
        send(zs_send, zs_recv.at[z], zs_ss.at[k], zs_rs.at[z], device(y, (z + k) % NZ, x, c), active)

    @pl.when(active)
    def _():
        for t in range(4):
            zs_recv[z, t] = zs_send[t]
        for k in range(1, 8):
            source = (z + k) % NZ
            arrive(zs_recv.at[source], zs_ss.at[0], zs_rs.at[source])
        slab = [None] * NS
        for zz in range(NZ):
            for t in range(2):
                for at, tile in ((entry_window(zz) + t, zs_recv[zz, t]), (6 + exit_window(zz) + t, zs_recv[zz, 2 + t])):
                    slab[at] = tile if slab[at] is None else slab[at] + tile
        for t in range(NS):
            s_all[x, y * NS + t] = slab[t]

    def gather(whole, n, ys, yr, xs, xr, cs, cr, use):
        def part(group, slab):
            return whole.at[group, pl.ds(slab * n, n)]

        def full(slab):
            return whole.at[:, pl.ds(slab * n, n)]

        for k in range(1, 8):
            send(part(x, y), part(x, y), ys.at[k], yr.at[y], device((y + k) % NY, z, x, c), active)
        for j in range(HALF):
            at = (y + j) % HALF
            slab = HALF * c + at
            arrive(part(x, slab), ys.at[0], yr.at[slab], slab != y)
            for k in range(1, 4):
                send(part(x, slab), part(x, slab), xs.at[j, k], xr.at[at, x], device(y, z, (x + k) % NX, c))
        for j in range(HALF):
            at = (y + j) % HALF
            slab = HALF * c + at
            for k in range(1, 4):
                source = (x + k) % NX
                arrive(part(source, slab), xs.at[0, 0], xr.at[at, source])
            send(full(slab), full(slab), cs.at[j], cr.at[at], other)
            use(slab)
        for j in range(HALF):
            at = (y + j) % HALF
            slab = HALF * (1 - c) + at
            arrive(full(slab), cs.at[0], cr.at[at])
            use(slab)

    def reduce(n, produce, between, local, from_core, from_x, y_send, from_y, cs, cr, xs, xr, ys, yr, result):
        for j in range(HALF):
            slab = HALF * (1 - c) + j
            produce(slab)
            send(local.at[:, pl.ds(slab * n, n)], from_core.at[:, pl.ds(j * n, n)], cs.at[j], cr.at[j], other)
        for j in range(HALF):
            slab = HALF * c + j
            produce(slab)
            arrive(from_core.at[:, pl.ds(j * n, n)], cs.at[0], cr.at[j])
            for g in range(GROUPS):
                for t in range(n):
                    local[g, slab * n + t] = local[g, slab * n + t] + from_core[g, j * n + t]
            for k in range(1, 4):
                to = (x + k) % NX
                send(
                    local.at[to, pl.ds(slab * n, n)], from_x.at[x, pl.ds(j * n, n)], xs.at[j, k], xr.at[j, x],
                    device(y, z, to, c),
                )
        between()
        for j in range(HALF):
            slab = HALF * c + j
            total = [local[x, slab * n + t] for t in range(n)]
            for k in range(1, 4):
                source = (x + k) % NX
                arrive(from_x.at[source, pl.ds(j * n, n)], xs.at[0, 0], xr.at[j, source])
                for t in range(n):
                    total[t] = total[t] + from_x[source, j * n + t]
            for t in range(n):
                y_send[j, t] = total[t]
            send(y_send.at[j], from_y.at[y], ys.at[j], yr.at[y], device(slab, z, x, c), slab != y)

        @pl.when(active)
        def _():
            total = [y_send[y % HALF, t] for t in range(n)]
            for k in range(1, 8):
                source = (y + k) % NY
                arrive(from_y.at[source], ys.at[0], yr.at[source])
                for t in range(n):
                    total[t] = total[t] + from_y[source, t]
            result(total)

    def tiles(whole, first, count):
        return jnp.concatenate(
            [jnp.concatenate([whole[g, first + t] for t in range(count)], axis=1) for g in range(GROUPS)], axis=0
        )

    def lanes(ref, slab, width):
        return ref[:, pl.ds(pl.multiple_of(slab * width, 128), width)]

    def contract(whole, first, count, weights, slab):
        pieces = split3(tiles(whole, first, count))
        part = lax.dot_general(pieces, lanes(weights, slab, 128 * count), NT, preferred_element_type=F32)
        return fold3(part), pieces

    def expand(pieces, weights, slab, count, whole, first):
        part = fold3(lax.dot_general(pieces, lanes(weights, slab, 128 * count), NN, preferred_element_type=F32))
        for g in range(GROUPS):
            for t in range(count):
                whole[g, first + t] = part[8 * g:8 * g + 8, 128 * t:128 * t + 128]

    for copy in loads:
        copy.wait()

    sums = {"entry": jnp.zeros((32, TOK), F32), "exit": jnp.zeros((32, TOK), F32)}

    def use_start(slab):
        sums["entry"] += contract(s_all, slab * NS, 6, wge, slab)[0]
        sums["exit"] += contract(s_all, slab * NS + 6, 3, wgx, slab)[0]

    gather(s_all, NS, sg_ys, sg_yr, sg_xs, sg_xr, sg_cs, sg_cr, use_start)
    left_entry, left_exit = split3(sums["entry"]), split3(sums["exit"])

    def produce_left(slab):
        expand(left_entry, wxe, slab, 3, l_loc, slab * NL)
        expand(left_exit, wxx, slab, 4, l_loc, slab * NL + 3)

    def left_result(total):
        for t in range(NL):
            l_zs[t] = total[t]

    reduce(
        NL, produce_left, lambda: None, l_loc, l_core, l_x, l_ys, l_y,
        lr_cs, lr_cr, lr_xs, lr_xr, lr_ys, lr_yr, left_result,
    )
    for k in range(1, 8):
        send(l_zs, l_z.at[z], lz_ss.at[k], lz_rs.at[z], device(y, (z + k) % NZ, x, c), active)

    @pl.when(active)
    def _():
        for t in range(NL):
            l_z[z, t] = l_zs[t]
        for k in range(1, 8):
            source = (z + k) % NZ
            arrive(l_z.at[source], lz_ss.at[0], lz_rs.at[source])
        for t in range(NL):
            total = l_z[0, t]
            for zz in range(1, NZ):
                total = total + l_z[zz, t]
            l_all[x, y * NL + t] = total

    sides = {"entry": jnp.zeros((32, TOK), F32), "exit": jnp.zeros((32, TOK), F32)}
    grams = {"entry": jnp.zeros((32, 96), F32), "exit": jnp.zeros((32, 96), F32)}

    def use_left(slab):
        for name, first, count, weights in (("entry", 0, 3, wxe), ("exit", 3, 4, wxx)):
            part, pieces = contract(l_all, slab * NL + first, count, weights, slab)
            sides[name] += part
            grams[name] += fold3(lax.dot_general(pieces, pieces, NT, preferred_element_type=F32))

    gather(l_all, NL, lg_ys, lg_yr, lg_xs, lg_xr, lg_cs, lg_cr, use_left)
    right_entry, right_exit = split3(sides["entry"]), split3(sides["exit"])

    def produce_right(slab):
        expand(right_entry, wge, slab, 6, f_loc, slab * NS)
        expand(right_exit, wgx, slab, 3, f_loc, slab * NS + 6)

    inverse = {}

    def cholesky():
        row, column = iota((32, 32), 0), iota((32, 32), 1)
        state = {}
        for name in ("entry", "exit"):
            gram = grams[name]
            state[name] = [
                gram[:, 0:32] + gram[:, 32:64] + gram[:, 64:96],
                jnp.where(row == column, 1.0, 0.0).astype(F32),
                jnp.ones((32, 1), F32),
            ]
        rows = iota((32, 1), 0)
        for j in range(32):
            for name in ("entry", "exit"):
                left, unit, diagonal = state[name]
                pivot = left[j:j + 1, j:j + 1]
                factor = jnp.where(rows > j, left[:, j:j + 1] / pivot, 0.0)
                state[name] = [
                    left - factor * left[j:j + 1, :],
                    unit - factor * unit[j:j + 1, :],
                    jnp.where(rows == j, pivot, diagonal),
                ]
        for name in ("entry", "exit"):
            inverse[name] = state[name][1] / jnp.sqrt(state[name][2])
        for name, first, count, each, put, width in (("entry", 0, 3, 6, 0, 3072), ("exit", 3, 4, 8, 8, 4096)):
            shape = (8, 128 * count)
            at = each * (8 * z + spot)
            pick = jnp.where((iota(shape, 1) == at + iota(shape, 0)) & (iota(shape, 0) < each), 1.0, 0.0).astype(F32)
            own = exact_dot(pick, tiles(l_all, y * NL + first, count), NT)
            out[put:put + 8, :] = exact_dot(own, inverse[name], NT) * math.sqrt(width)

    def right_result(total):
        for zz in range(NZ):
            for t in range(2):
                f_zs[zz, t] = total[entry_window(zz) + t]
                f_zs[zz, 2 + t] = total[6 + exit_window(zz) + t]

    reduce(
        NS, produce_right, cholesky, f_loc, f_core, f_x, f_ys, f_y,
        fr_cs, fr_cr, fr_xs, fr_xr, fr_ys, fr_yr, right_result,
    )
    for k in range(1, 8):
        to = (z + k) % NZ
        send(f_zs.at[to], f_z.at[z], fz_ss.at[k], fz_rs.at[z], device(y, to, x, c), active)

    @pl.when(active)
    def _():
        total = [f_zs[z, t] for t in range(4)]
        for k in range(1, 8):
            source = (z + k) % NZ
            arrive(f_z.at[source], fz_ss.at[0], fz_rs.at[source])
            for t in range(4):
                total[t] = total[t] + f_z[source, t]
        for t in range(4):
            f_own[t] = total[t]

    for k in range(1, 8):
        send(
            f_own, f_last.at[x], last_ss.at[k], last_rs.at[x],
            device(y, z, (x + k // 2) % NX, (c + k) % 2), active,
        )

    @pl.when(active)
    def _():
        for t in range(4):
            f_last[x, t] = f_own[t]

    for k in range(4):
        source = (x + k) % NX
        arrive(f_last.at[source], last_ss.at[0], last_rs.at[source], jnp.logical_not(active) if k == 0 else None)
    for name, first, pick, put in (("entry", 0, pick_entry, 16), ("exit", 2, pick_exit, 32)):
        own = exact_dot(pick, tiles(f_last, first, 2), NT)
        out[put:put + 16, :] = exact_dot(own, inverse[name], NT) * (1.0 / 512)

    for cond, copy in pending:
        guarded(cond, copy.wait_send)


def outputs_kernel(packed, entry_basis, exit_basis, entry_factor, exit_factor):
    entry_basis[...] = packed[0:6, :]
    exit_basis[...] = packed[8:16, :]
    entry_factor[...] = packed[16:28, :]
    exit_factor[...] = packed[32:38, :]


def body(*args):
    dma = pltpu.SemaphoreType.DMA
    tile = (8, 128)

    def f32(*shape):
        return pltpu.VMEM(shape + tile, F32)

    def reduce_buffers(n):
        return [f32(4, 8 * n), f32(4, 4 * n), f32(4, 4 * n), f32(4, n), f32(8, n)]

    scratch = [
        pltpu.VMEM((TOK, 3072), BF16), pltpu.VMEM((TOK, 6144), BF16),
        pltpu.VMEM((TOK, 4096), BF16), pltpu.VMEM((TOK, 3072), BF16),
        pltpu.VMEM((32, 32), F32),
        f32(4, 8 * NS), f32(4, 8 * NL),
        f32(4, 4), f32(8, 4), f32(4), f32(8, 4),
        *reduce_buffers(NL), f32(NL), f32(8, NL),
        *reduce_buffers(NS), f32(8, 4), f32(8, 4), f32(4, 4), f32(4),
        dma((8,)),
        dma((4,)), dma((8,)), dma((8,)), dma((8,)), dma((8,)), dma((8,)), dma((8,)), dma((8,)), dma((8,)), dma((4,)),
    ]
    for _ in range(2):
        scratch += [dma((8,)), dma((8,)), dma((4, 4)), dma((4, 4)), dma((4,)), dma((4,))]
    for _ in range(2):
        scratch += [dma((4,)), dma((4,)), dma((4, 4)), dma((4, 4)), dma((4,)), dma((8,))]
    vmem = pl.BlockSpec(memory_space=pltpu.VMEM)
    anywhere = pl.BlockSpec(memory_space=pltpu.HBM)
    packed = pl.pallas_call(
        kernel,
        out_shape=jax.ShapeDtypeStruct((48, 32), F32),
        in_specs=[anywhere] * 8 + [vmem] * 2,
        out_specs=vmem,
        scratch_shapes=scratch,
        compiler_params=pltpu.CompilerParams(
            collective_id=0, has_side_effects=True, vmem_limit_bytes=48 * 1024 * 1024
        ),
        name="powersgd",
    )(*args)
    return pl.pallas_call(
        outputs_kernel,
        out_shape=tuple(jax.ShapeDtypeStruct((rows, 32), F32) for rows in (6, 8, 12, 6)),
        in_specs=[vmem],
        out_specs=(vmem,) * 4,
        name="outputs",
    )(packed)


def solution(mesh):
    spec = P("dp", None)
    return jax.shard_map(body, mesh=mesh, in_specs=(spec,) * 10, out_specs=(spec,) * 4, check_vma=False)
```

```python
import math

import jax
import jax.numpy as jnp
from jax import lax
from jax.experimental import pallas as pl
from jax.experimental.pallas import tpu as pltpu
from jax.sharding import PartitionSpec as P

MESH = pl.DeviceIdType.MESH
NY, NZ, NX = 8, 8, 4
GROUPS = 4
HALF = 4
FAR = (4, 3, 5, 2, 6, 1, 7)
FAR_X = (2, 1, 3)
TOK = 144
F32 = jnp.float32
BF16 = jnp.bfloat16
NT = (((1,), (1,)), ((), ()))
NN = (((1,), (0,)), ((), ()))
TN = (((0,), (0,)), ((), ()))


class Matrix:
    def __init__(self, width, outs, put_basis, put_factor):
        self.width, self.outs = width, outs
        self.nl, self.ns = width // (NY * 128), outs // (NY * 128)
        self.left_rows, self.right_rows = width // 512, outs // 512
        self.lanes = outs // (NY * NZ)
        self.put_basis, self.put_factor = put_basis, put_factor


ENTRY = Matrix(3072, 6144, 0, 16)
EXIT = Matrix(4096, 3072, 8, 32)


def device(y, z, x, c):
    return ((y * NZ + z) * NX + x) * 2 + c


def split3(v):
    hi = v.astype(BF16)
    rest = v - hi.astype(F32)
    mid = rest.astype(BF16)
    lo = (rest - mid.astype(F32)).astype(BF16)
    return jnp.concatenate([hi, mid, lo], axis=0)


def fold3(v):
    return v[0:32] + v[32:64] + v[64:96]


def exact_dot(a, b, dims):
    return lax.dot_general(a, b, dims, precision=lax.Precision.HIGHEST, preferred_element_type=F32)


def iota(shape, dim):
    return lax.broadcasted_iota(jnp.int32, shape, dim)


def kernel(
    entry_input, entry_grad, exit_input, exit_grad,
    entry_left, entry_right, exit_left, exit_right,
    entry_start, exit_start,
    out, load_sem, entry_scratch, exit_scratch,
):
    me = lax.axis_index("dp")
    y, z, x, c = me // (NZ * NX * 2), (me // (NX * 2)) % NZ, (me // 2) % NX, me % 2
    active_core = y // HALF
    active = c == active_core
    passive = c != active_core
    other = device(y, z, x, 1 - c)
    spot = 2 * x + c
    pair = (y // 2) % 2
    issued = [[]]

    def remote(src, dst, ss, rs, target):
        return pltpu.make_async_remote_copy(
            src_ref=src, dst_ref=dst, send_sem=ss, recv_sem=rs, device_id=(target,), device_id_type=MESH
        )

    def guarded(cond, fn):
        if cond is None:
            fn()
        else:
            @pl.when(cond)
            def _():
                fn()

    def send(copies, ss, moved, cond=None):
        def start():
            for src, dst, rs, target in copies:
                remote(src, dst, ss, rs, target).start()

        guarded(cond, start)
        issued[-1].append((cond, remote(moved, moved, ss, ss, other)))

    def arrive(dst, rs, cond=None):
        guarded(cond, remote(dst, dst, rs, rs, other).wait_recv)

    def drain(rounds):
        while len(issued) > rounds:
            for cond, copy in issued.pop(0):
                guarded(cond, copy.wait_send)

    barrier = pltpu.get_barrier_semaphore()
    peers = [device(y, z, (x + k // 2) % NX, (c + k) % 2) for k in range(1, 8)]
    peers += [device(y, (z + k) % NZ, x, c) for k in range(1, 8)]
    peers += [device((y + k) % NY, z, x, c) for k in range(1, 8)]
    for peer in peers:
        pl.semaphore_signal(barrier, inc=1, device_id=(peer,), device_id_type=MESH)

    loads = []
    for i, (src, dst, row, rows) in enumerate((
        (entry_grad, entry_scratch["wg"], 0, 128), (entry_right, entry_scratch["wg"], 128, 16),
        (exit_grad, exit_scratch["wg"], 0, 128), (exit_right, exit_scratch["wg"], 128, 16),
        (entry_input, entry_scratch["wx"], 0, 128), (entry_left, entry_scratch["wx"], 128, 16),
        (exit_input, exit_scratch["wx"], 0, 128), (exit_left, exit_scratch["wx"], 128, 16),
    )):
        copy = pltpu.make_async_copy(src, dst.at[pl.ds(row, rows)], load_sem.at[i])
        copy.start()
        loads.append(copy)

    def tiles(whole, first, count):
        return jnp.concatenate(
            [jnp.concatenate([whole[g, first + t] for t in range(count)], axis=1) for g in range(GROUPS)], axis=0
        )

    def columns(ref, slab, count):
        return ref[:, pl.ds(pl.multiple_of(slab * (128 * count), 128), 128 * count)]

    def contract(whole, n, weights, slab):
        pieces = split3(tiles(whole, slab * n, n))
        part = lax.dot_general(pieces, columns(weights, slab, n), NT, preferred_element_type=F32)
        return fold3(part), pieces

    def expand(pieces, weights, slab, n, whole):
        part = fold3(lax.dot_general(pieces, columns(weights, slab, n), NN, preferred_element_type=F32))
        for g in range(GROUPS):
            for t in range(n):
                whole[g, slab * n + t] = part[8 * g:8 * g + 8, 128 * t:128 * t + 128]

    def batches(half, far_first):
        near = jnp.where(half == active_core, pair, 1 - pair)
        first = 1 - near if far_first else near
        return [(b, HALF * half + 2 * b) for b in (first, 1 - first)]

    def gather(whole, n, sems, moved, use):
        ys, yr, xs, xr, cs, cr = sems

        def part(group, slab, count):
            return whole.at[group, pl.ds(slab * n, count * n)]

        def full(slab):
            return whole.at[:, pl.ds(slab * n, 2 * n)]

        mine = part(x, y, 1)
        send(
            [(mine, mine, yr.at[(y // 2) % 2], device((y + k) % NY, z, x, c)) for k in FAR],
            ys, moved.at[pl.ds(0, 7)], active,
        )
        yield
        for b, slab in batches(c, False):
            own = active & (b == pair)
            arrive(part(x, slab, 1), yr.at[b], own)
            arrive(part(x, slab, 2), yr.at[b], jnp.logical_not(own))
            both = part(x, slab, 2)
            send(
                [(both, both, xr.at[b], device(y, z, (x + k) % NX, c)) for k in FAR_X],
                xs.at[b], whole.at[pl.ds(0, 3), pl.ds(0, 2 * n)],
            )
        yield
        for b, slab in batches(c, False):
            arrive(whole.at[pl.ds(0, 3), pl.ds(0, 2 * n)], xr.at[b])
            send([(full(slab), full(slab), cr.at[b], other)], cs.at[b], full(slab))
        for b, slab in batches(c, False):
            use(slab)
            use(slab + 1)
        yield
        for b, slab in batches(1 - c, False):
            arrive(full(slab), cr.at[b])
            use(slab)
            use(slab + 1)

    def reduce(n, pieces, weights, buffers, sems):
        local, from_core, from_x, y_send, from_y = buffers
        cs, cr, xs, xr, ys, yr = sems
        for b, slab in batches(1 - c, True):
            expand(pieces, weights, slab, n, local)
            expand(pieces, weights, slab + 1, n, local)
            src = local.at[:, pl.ds(slab * n, 2 * n)]
            send([(src, from_core.at[:, pl.ds(2 * b * n, 2 * n)], cr.at[b], other)], cs.at[b], src)
        for b, slab in batches(c, True):
            expand(pieces, weights, slab, n, local)
            expand(pieces, weights, slab + 1, n, local)
        yield
        for b, slab in batches(c, True):
            arrive(from_core.at[:, pl.ds(2 * b * n, 2 * n)], cr.at[b])
            for g in range(GROUPS):
                for t in range(2 * n):
                    local[g, slab * n + t] = local[g, slab * n + t] + from_core[g, 2 * b * n + t]
            send(
                [
                    (
                        local.at[(x + k) % NX, pl.ds(slab * n, 2 * n)], from_x.at[x, pl.ds(2 * b * n, 2 * n)],
                        xr.at[b], device(y, z, (x + k) % NX, c),
                    )
                    for k in FAR_X
                ],
                xs.at[b], from_x.at[pl.ds(0, 3), pl.ds(0, 2 * n)],
            )
        yield
        for b, slab in batches(c, True):
            arrive(from_x.at[pl.ds(0, 3), pl.ds(0, 2 * n)], xr.at[b])
            for i in range(2):
                for t in range(n):
                    total = local[x, (slab + i) * n + t]
                    for k in range(1, 4):
                        total = total + from_x[(x + k) % NX, (2 * b + i) * n + t]
                    y_send[2 * b + i, t] = total
                copy = remote(
                    y_send.at[2 * b + i], from_y.at[y], ys, yr, device(slab + i, z, x, c)
                )
                guarded(slab + i != y, copy.start)
        issued[-1].append((active, remote(from_y.at[pl.ds(0, 3)], from_y.at[pl.ds(0, 3)], ys, ys, other)))
        issued[-1].append((passive, remote(from_y.at[pl.ds(0, 4)], from_y.at[pl.ds(0, 4)], ys, ys, other)))
        yield

    def summed_over_y(n, buffers, sems):
        y_send, from_y = buffers[3:]
        arrive(from_y.at[pl.ds(0, 7)], sems[5])
        total = [y_send[y % HALF, t] for t in range(n)]
        for k in range(1, 8):
            for t in range(n):
                total[t] = total[t] + from_y[(y + k) % NY, t]
        return total

    lane = iota((8, 128), 1)
    grams, inverse = {}, {}

    def chain(m, start, s, load_g, load_x):
        rows = m.right_rows
        s["own"][...] = jnp.zeros_like(s["own"])
        s["own"][0:rows, :] = start[...]
        at = m.lanes * z + rows * spot
        pick = jnp.where(
            (iota((16, 128), 1) == (at + iota((16, 128), 0)) % 128) & (iota((16, 128), 0) < rows), 1.0, 0.0
        ).astype(F32)
        placed = exact_dot(s["own"][...], pick, TN)
        for g in range(GROUPS):
            s["first_send"][g] = placed[8 * g:8 * g + 8, :]
        yield
        first_ss, first_rs = s["first_sems"]
        landing = s["first_recv"].at[spot]
        send([(s["first_send"].at[x], landing, first_rs, other)], first_ss.at[0], s["first_send"].at[0], passive)
        send(
            [
                (s["first_send"].at[(x + k) % NX], landing, first_rs, device(y, z, (x + k) % NX, active_core))
                for k in FAR_X
            ],
            first_ss.at[1], s["first_send"].at[pl.ds(0, 3)],
        )
        yield

        @pl.when(active)
        def _():
            arrive(s["first_recv"].at[pl.ds(0, 7)], first_rs)
            total = s["first_send"][x]
            for k in range(1, 8):
                total = total + s["first_recv"][(spot + k) % 8]
            s["zs_send"][...] = total

        zs_ss, zs_rs = s["zs_sems"]
        send(
            [(s["zs_send"], s["zs_recv"].at[z], zs_rs, device(y, (z + k) % NZ, x, c)) for k in FAR],
            zs_ss, s["zs_recv"].at[pl.ds(0, 7)], active,
        )
        yield

        @pl.when(active)
        def _():
            s["zs_recv"][z] = s["zs_send"][...]
            arrive(s["zs_recv"].at[pl.ds(0, 7)], zs_rs)
            slab = [jnp.zeros((8, 128), F32) for _ in range(m.ns)]
            for zz in range(NZ):
                t, first = divmod(m.lanes * zz, 128)
                piece = s["zs_recv"][zz]
                if first + m.lanes <= 128:
                    slab[t] = slab[t] + piece
                else:
                    slab[t] = slab[t] + jnp.where(lane >= first, piece, 0.0)
                    slab[t + 1] = slab[t + 1] + jnp.where(lane < first, piece, 0.0)
            for t in range(m.ns):
                s["s_all"][x, y * m.ns + t] = slab[t]

        for copy in load_g:
            copy.wait()
        total = [jnp.zeros((32, TOK), F32)]

        def use_start(slab):
            total[0] += contract(s["s_all"], m.ns, s["wg"], slab)[0]

        yield from gather(s["s_all"], m.ns, s["s_gather"], s["f_buffers"][4], use_start)
        left = split3(total[0])
        for copy in load_x:
            copy.wait()
        yield from reduce(m.nl, left, s["wx"], s["l_buffers"], s["l_reduce"])

        @pl.when(active)
        def _():
            total = summed_over_y(m.nl, s["l_buffers"], s["l_reduce"])
            for t in range(m.nl):
                s["l_zs"][t] = total[t]

        lz_ss, lz_rs = s["lz_sems"]
        send(
            [(s["l_zs"], s["l_z"].at[z], lz_rs, device(y, (z + k) % NZ, x, c)) for k in FAR],
            lz_ss, s["l_z"].at[pl.ds(0, 7)], active,
        )
        yield

        @pl.when(active)
        def _():
            for t in range(m.nl):
                s["l_z"][z, t] = s["l_zs"][t]
            arrive(s["l_z"].at[pl.ds(0, 7)], lz_rs)
            for t in range(m.nl):
                total = s["l_z"][0, t]
                for zz in range(1, NZ):
                    total = total + s["l_z"][zz, t]
                s["l_all"][x, y * m.nl + t] = total

        side = [jnp.zeros((32, TOK), F32), jnp.zeros((32, 96), F32)]

        def use_left(slab):
            part, pieces = contract(s["l_all"], m.nl, s["wx"], slab)
            side[0] += part
            side[1] += fold3(lax.dot_general(pieces, pieces, NT, preferred_element_type=F32))

        yield from gather(s["l_all"], m.nl, s["l_gather"], s["l_z"], use_left)
        grams[m] = side[1]
        right = split3(side[0])
        yield from reduce(m.ns, right, s["wg"], s["f_buffers"], s["f_reduce"])

        @pl.when(active)
        def _():
            total = summed_over_y(m.ns, s["f_buffers"], s["f_reduce"])
            for zz in range(NZ):
                t, first = divmod(m.lanes * zz, 128)
                if first + m.lanes <= 128:
                    s["f_zs"][zz] = total[t]
                else:
                    s["f_zs"][zz] = jnp.where(lane >= first, total[t], total[t + 1])

        fz_ss, fz_rs = s["fz_sems"]
        send(
            [(s["f_zs"].at[(z + k) % NZ], s["f_z"].at[z], fz_rs, device(y, (z + k) % NZ, x, c)) for k in FAR],
            fz_ss, s["f_z"].at[pl.ds(0, 7)], active,
        )
        yield

        @pl.when(active)
        def _():
            arrive(s["f_z"].at[pl.ds(0, 7)], fz_rs)
            total = s["f_zs"][z]
            for k in range(1, 8):
                total = total + s["f_z"][(z + k) % NZ]
            s["f_own"][...] = total

        last_ss, last_rs = s["last_sems"]
        send(
            [
                (s["f_own"], s["f_last"].at[x], last_rs, device(y, z, (x + k // 2) % NX, (c + k) % 2))
                for k in (4, 5, 2, 3, 6, 7, 1)
            ],
            last_ss, s["f_z"].at[pl.ds(0, 7)], active,
        )

        @pl.when(active)
        def _():
            s["f_last"][x] = s["f_own"][...]

        yield
        arrive(s["f_last"].at[pl.ds(0, 3)], last_rs, active)
        arrive(s["f_last"], last_rs, passive)
        raw = jnp.concatenate([s["f_last"][g] for g in range(GROUPS)], axis=0)
        own = exact_dot(pick, raw, NT)
        out[m.put_factor:m.put_factor + 16, :] = exact_dot(own, inverse[m], NT) * (1.0 / 512)

    def cholesky():
        row, column = iota((32, 32), 0), iota((32, 32), 1)
        rows = iota((32, 1), 0)
        state = {}
        for m in (ENTRY, EXIT):
            gram = grams[m]
            state[m] = [
                gram[:, 0:32] + gram[:, 32:64] + gram[:, 64:96],
                jnp.where(row == column, 1.0, 0.0).astype(F32),
                jnp.ones((32, 1), F32),
            ]
        for j in range(32):
            for m in (ENTRY, EXIT):
                left, unit, diagonal = state[m]
                pivot = left[j:j + 1, j:j + 1]
                factor = jnp.where(rows > j, left[:, j:j + 1] / pivot, 0.0)
                state[m] = [
                    left - factor * left[j:j + 1, :],
                    unit - factor * unit[j:j + 1, :],
                    jnp.where(rows == j, pivot, diagonal),
                ]
            if j % 11 == 10:
                yield
        for m, s in ((ENTRY, entry_scratch), (EXIT, exit_scratch)):
            inverse[m] = state[m][1] / jnp.sqrt(state[m][2])
            shape = (8, 128 * m.nl)
            at = m.left_rows * (8 * z + spot)
            pick = jnp.where(
                (iota(shape, 1) == at + iota(shape, 0)) & (iota(shape, 0) < m.left_rows), 1.0, 0.0
            ).astype(F32)
            own = exact_dot(pick, tiles(s["l_all"], y * m.nl, m.nl), NT)
            out[m.put_basis:m.put_basis + 8, :] = exact_dot(own, inverse[m], NT) * math.sqrt(m.width)
        yield

    chains = [
        chain(ENTRY, entry_start, entry_scratch, loads[0:2], loads[4:6]),
        chain(EXIT, exit_start, exit_scratch, loads[2:4], loads[6:8]),
    ]
    for step in chains:
        next(step)
    pl.semaphore_wait(barrier, len(peers))
    extra = None
    while chains:
        issued.append([])
        chains = [step for step in chains if next(step, chains) is None]
        drain(2)
        if extra is None and len(grams) == 2:
            extra = cholesky()
        elif extra is not None:
            next(extra, None)
    drain(0)


def outputs_kernel(packed, entry_basis, exit_basis, entry_factor, exit_factor):
    entry_basis[...] = packed[0:6, :]
    exit_basis[...] = packed[8:16, :]
    entry_factor[...] = packed[16:28, :]
    exit_factor[...] = packed[32:38, :]


def scratch_of(m):
    dma = pltpu.SemaphoreType.DMA

    def f32(*shape):
        return pltpu.VMEM(shape + (8, 128), F32)

    def gather_sems():
        return [dma, dma((2,)), dma((2,)), dma((2,)), dma((2,)), dma((2,))]

    def reduce_sems():
        return [dma((2,)), dma((2,)), dma((2,)), dma((2,)), dma, dma]

    def reduce_buffers(n):
        return [f32(4, 8 * n), f32(4, 4 * n), f32(4, 4 * n), f32(4, n), f32(8, n)]

    return {
        "wg": pltpu.VMEM((TOK, m.outs), BF16),
        "wx": pltpu.VMEM((TOK, m.width), BF16),
        "own": pltpu.VMEM((16, 32), F32),
        "first_send": f32(4), "first_recv": f32(8), "first_sems": [dma((2,)), dma],
        "zs_send": f32(), "zs_recv": f32(8), "zs_sems": [dma, dma],
        "s_all": f32(4, 8 * m.ns), "s_gather": gather_sems(),
        "l_buffers": reduce_buffers(m.nl), "l_reduce": reduce_sems(),
        "l_zs": f32(m.nl), "l_z": f32(8, m.nl), "lz_sems": [dma, dma],
        "l_all": f32(4, 8 * m.nl), "l_gather": gather_sems(),
        "f_buffers": reduce_buffers(m.ns), "f_reduce": reduce_sems(),
        "f_zs": f32(8), "f_z": f32(8), "fz_sems": [dma, dma],
        "f_own": f32(), "f_last": f32(4), "last_sems": [dma, dma],
    }


def body(*args):
    vmem = pl.BlockSpec(memory_space=pltpu.VMEM)
    hbm = pl.BlockSpec(memory_space=pltpu.HBM)
    packed = pl.pallas_call(
        kernel,
        out_shape=jax.ShapeDtypeStruct((48, 32), F32),
        in_specs=[hbm] * 8 + [vmem] * 2,
        out_specs=vmem,
        scratch_shapes=[pltpu.SemaphoreType.DMA((8,)), scratch_of(ENTRY), scratch_of(EXIT)],
        compiler_params=pltpu.CompilerParams(
            collective_id=0, has_side_effects=True, vmem_limit_bytes=63 * 1024 * 1024
        ),
        name="powersgd",
    )(*args)
    return pl.pallas_call(
        outputs_kernel,
        out_shape=tuple(jax.ShapeDtypeStruct((rows, 32), F32) for rows in (6, 8, 12, 6)),
        in_specs=[vmem],
        out_specs=(vmem,) * 4,
        name="outputs",
    )(packed)


def solution(mesh):
    spec = P("dp", None)
    return jax.shard_map(body, mesh=mesh, in_specs=(spec,) * 10, out_specs=(spec,) * 4, check_vma=False)
```

```python
import math

import jax
import jax.numpy as jnp
from jax import lax
from jax.experimental import pallas as pl
from jax.experimental.pallas import tpu as pltpu
from jax.sharding import PartitionSpec as P

MESH = pl.DeviceIdType.MESH
NY, NZ, NX = 8, 8, 4
GROUPS = 4
HALF = 4
FAR = (4, 3, 5, 2, 6, 1, 7)
FAR_X = (2, 1, 3)
TOK = 144
F32 = jnp.float32
BF16 = jnp.bfloat16
NT = (((1,), (1,)), ((), ()))
NN = (((1,), (0,)), ((), ()))
TN = (((0,), (0,)), ((), ()))


class Matrix:
    def __init__(self, width, outs, put_basis, put_factor):
        self.width, self.outs = width, outs
        self.nl, self.ns = width // (NY * 128), outs // (NY * 128)
        self.left_rows, self.right_rows = width // 512, outs // 512
        self.lanes = outs // (NY * NZ)
        self.put_basis, self.put_factor = put_basis, put_factor


ENTRY = Matrix(3072, 6144, 0, 16)
EXIT = Matrix(4096, 3072, 8, 32)


def device(y, z, x, c):
    return ((y * NZ + z) * NX + x) * 2 + c


def split3(v):
    hi = v.astype(BF16)
    rest = v - hi.astype(F32)
    mid = rest.astype(BF16)
    lo = (rest - mid.astype(F32)).astype(BF16)
    return jnp.concatenate([hi, mid, lo], axis=0)


def fold3(v):
    return v[0:32] + v[32:64] + v[64:96]


def exact_dot(a, b, dims):
    return lax.dot_general(a, b, dims, precision=lax.Precision.HIGHEST, preferred_element_type=F32)


def iota(shape, dim):
    return lax.broadcasted_iota(jnp.int32, shape, dim)


def kernel(
    entry_input, entry_grad, exit_input, exit_grad,
    entry_left, entry_right, exit_left, exit_right,
    entry_start, exit_start,
    out, load_sem, entry_scratch, exit_scratch,
):
    me = lax.axis_index("dp")
    y, z, x, c = me // (NZ * NX * 2), (me // (NX * 2)) % NZ, (me // 2) % NX, me % 2
    active_core = y // HALF
    active = c == active_core
    passive = c != active_core
    other = device(y, z, x, 1 - c)
    spot = 2 * x + c
    pair = (y // 2) % 2
    issued = [[]]

    def remote(src, dst, ss, rs, target):
        return pltpu.make_async_remote_copy(
            src_ref=src, dst_ref=dst, send_sem=ss, recv_sem=rs, device_id=(target,), device_id_type=MESH
        )

    def guarded(cond, fn):
        if cond is None:
            fn()
        else:
            @pl.when(cond)
            def _():
                fn()

    def send(copies, ss, moved, cond=None):
        def start():
            for src, dst, rs, target in copies:
                remote(src, dst, ss, rs, target).start()

        guarded(cond, start)
        issued[-1].append((cond, remote(moved, moved, ss, ss, other)))

    def arrive(dst, rs, cond=None):
        guarded(cond, remote(dst, dst, rs, rs, other).wait_recv)

    def drain(rounds):
        while len(issued) > rounds:
            for cond, copy in issued.pop(0):
                guarded(cond, copy.wait_send)

    barrier = pltpu.get_barrier_semaphore()
    peers = [device(y, z, (x + k // 2) % NX, (c + k) % 2) for k in range(1, 8)]
    peers += [device(y, (z + k) % NZ, x, c) for k in range(1, 8)]
    peers += [device((y + k) % NY, z, x, c) for k in range(1, 8)]
    for peer in peers:
        pl.semaphore_signal(barrier, inc=1, device_id=(peer,), device_id_type=MESH)

    starts = []
    for i, (src, s) in enumerate(((entry_start, entry_scratch), (exit_start, exit_scratch))):
        copy = pltpu.make_async_copy(src, s["start"], load_sem.at[8 + i])
        copy.start()
        starts.append(copy)
    loads = []
    for i, (src, dst, row, rows) in enumerate((
        (entry_grad, entry_scratch["wg"], 0, 128), (entry_right, entry_scratch["wg"], 128, 16),
        (exit_grad, exit_scratch["wg"], 0, 128), (exit_right, exit_scratch["wg"], 128, 16),
        (entry_input, entry_scratch["wx"], 0, 128), (entry_left, entry_scratch["wx"], 128, 16),
        (exit_input, exit_scratch["wx"], 0, 128), (exit_left, exit_scratch["wx"], 128, 16),
    )):
        copy = pltpu.make_async_copy(src, dst.at[pl.ds(row, rows)], load_sem.at[i])
        copy.start()
        loads.append(copy)

    def tiles(whole, first, count):
        return jnp.concatenate(
            [jnp.concatenate([whole[g, first + t] for t in range(count)], axis=1) for g in range(GROUPS)], axis=0
        )

    def columns(ref, slab, count):
        return ref[:, pl.ds(pl.multiple_of(slab * (128 * count), 128), 128 * count)]

    def contract(whole, n, weights, slab):
        pieces = split3(tiles(whole, slab * n, n))
        part = lax.dot_general(pieces, columns(weights, slab, n), NT, preferred_element_type=F32)
        return fold3(part), pieces

    def expand(pieces, weights, slab, n, whole):
        part = fold3(lax.dot_general(pieces, columns(weights, slab, n), NN, preferred_element_type=F32))
        for g in range(GROUPS):
            for t in range(n):
                whole[g, slab * n + t] = part[8 * g:8 * g + 8, 128 * t:128 * t + 128]

    def batches(half, far_first):
        near = jnp.where(half == active_core, pair, 1 - pair)
        first = 1 - near if far_first else near
        return [(b, HALF * half + 2 * b) for b in (first, 1 - first)]

    def gather(whole, n, sems, moved, use):
        ys, yr, xs, xr, cs, cr = sems

        def part(group, slab, count):
            return whole.at[group, pl.ds(slab * n, count * n)]

        def full(slab):
            return whole.at[:, pl.ds(slab * n, 2 * n)]

        mine = part(x, y, 1)
        send(
            [(mine, mine, yr.at[(y // 2) % 2], device((y + k) % NY, z, x, c)) for k in FAR],
            ys, moved.at[pl.ds(0, 7)], active,
        )
        yield
        for b, slab in batches(c, False):
            own = active & (b == pair)
            arrive(part(x, slab, 1), yr.at[b], own)
            arrive(part(x, slab, 2), yr.at[b], jnp.logical_not(own))
            both = part(x, slab, 2)
            send(
                [(both, both, xr.at[b], device(y, z, (x + k) % NX, c)) for k in FAR_X],
                xs.at[b], whole.at[pl.ds(0, 3), pl.ds(0, 2 * n)],
            )
        yield
        for b, slab in batches(c, False):
            arrive(whole.at[pl.ds(0, 3), pl.ds(0, 2 * n)], xr.at[b])
            send([(full(slab), full(slab), cr.at[b], other)], cs.at[b], full(slab))
        for b, slab in batches(c, False):
            use(slab)
            use(slab + 1)
        for b, slab in batches(1 - c, False):
            arrive(full(slab), cr.at[b])
            use(slab)
            use(slab + 1)

    def reduce(n, pieces, weights, buffers, sems):
        local, from_core, from_x, y_send, from_y = buffers
        cs, cr, xs, xr, ys, yr = sems
        for b, slab in batches(1 - c, True):
            expand(pieces, weights, slab, n, local)
            expand(pieces, weights, slab + 1, n, local)
            src = local.at[:, pl.ds(slab * n, 2 * n)]
            send([(src, from_core.at[:, pl.ds(2 * b * n, 2 * n)], cr.at[b], other)], cs.at[b], src)
        for b, slab in batches(c, True):
            expand(pieces, weights, slab, n, local)
            expand(pieces, weights, slab + 1, n, local)
        for b, slab in batches(c, True):
            arrive(from_core.at[:, pl.ds(2 * b * n, 2 * n)], cr.at[b])
            for g in range(GROUPS):
                for t in range(2 * n):
                    local[g, slab * n + t] = local[g, slab * n + t] + from_core[g, 2 * b * n + t]
            send(
                [
                    (
                        local.at[(x + k) % NX, pl.ds(slab * n, 2 * n)], from_x.at[x, pl.ds(2 * b * n, 2 * n)],
                        xr.at[b], device(y, z, (x + k) % NX, c),
                    )
                    for k in FAR_X
                ],
                xs.at[b], from_x.at[pl.ds(0, 3), pl.ds(0, 2 * n)],
            )
        yield
        for b, slab in batches(c, True):
            arrive(from_x.at[pl.ds(0, 3), pl.ds(0, 2 * n)], xr.at[b])
            for i in range(2):
                for t in range(n):
                    total = local[x, (slab + i) * n + t]
                    for k in range(1, 4):
                        total = total + from_x[(x + k) % NX, (2 * b + i) * n + t]
                    y_send[2 * b + i, t] = total
                copy = remote(
                    y_send.at[2 * b + i], from_y.at[y], ys, yr, device(slab + i, z, x, c)
                )
                guarded(slab + i != y, copy.start)
        issued[-1].append((active, remote(from_y.at[pl.ds(0, 3)], from_y.at[pl.ds(0, 3)], ys, ys, other)))
        issued[-1].append((passive, remote(from_y.at[pl.ds(0, 4)], from_y.at[pl.ds(0, 4)], ys, ys, other)))
        yield

    def summed_over_y(n, buffers, sems):
        y_send, from_y = buffers[3:]
        arrive(from_y.at[pl.ds(0, 7)], sems[5])
        total = [y_send[y % HALF, t] for t in range(n)]
        for k in range(1, 8):
            for t in range(n):
                total[t] = total[t] + from_y[(y + k) % NY, t]
        return total

    lane = iota((8, 128), 1)
    grams, inverse = {}, {}

    def chain(m, start, s, load_g, load_x):
        rows = m.right_rows
        s["own"][...] = jnp.zeros_like(s["own"])
        start.wait()
        s["own"][0:rows, :] = s["start"][...]
        at = m.lanes * z + rows * spot
        pick = jnp.where(
            (iota((16, 128), 1) == (at + iota((16, 128), 0)) % 128) & (iota((16, 128), 0) < rows), 1.0, 0.0
        ).astype(F32)
        placed = exact_dot(s["own"][...], pick, TN)
        for g in range(GROUPS):
            s["first_send"][g] = placed[8 * g:8 * g + 8, :]
        yield
        first_ss, first_rs = s["first_sems"]
        landing = s["first_recv"].at[spot]
        send([(s["first_send"].at[x], landing, first_rs, other)], first_ss.at[0], s["first_send"].at[0], passive)
        send(
            [
                (s["first_send"].at[(x + k) % NX], landing, first_rs, device(y, z, (x + k) % NX, active_core))
                for k in FAR_X
            ],
            first_ss.at[1], s["first_send"].at[pl.ds(0, 3)],
        )
        yield

        @pl.when(active)
        def _():
            arrive(s["first_recv"].at[pl.ds(0, 7)], first_rs)
            total = s["first_send"][x]
            for k in range(1, 8):
                total = total + s["first_recv"][(spot + k) % 8]
            s["zs_send"][...] = total

        zs_ss, zs_rs = s["zs_sems"]
        send(
            [(s["zs_send"], s["zs_recv"].at[z], zs_rs, device(y, (z + k) % NZ, x, c)) for k in FAR],
            zs_ss, s["zs_recv"].at[pl.ds(0, 7)], active,
        )
        yield

        @pl.when(active)
        def _():
            s["zs_recv"][z] = s["zs_send"][...]
            arrive(s["zs_recv"].at[pl.ds(0, 7)], zs_rs)
            slab = [jnp.zeros((8, 128), F32) for _ in range(m.ns)]
            for zz in range(NZ):
                t, first = divmod(m.lanes * zz, 128)
                piece = s["zs_recv"][zz]
                if first + m.lanes <= 128:
                    slab[t] = slab[t] + piece
                else:
                    slab[t] = slab[t] + jnp.where(lane >= first, piece, 0.0)
                    slab[t + 1] = slab[t + 1] + jnp.where(lane < first, piece, 0.0)
            for t in range(m.ns):
                s["s_all"][x, y * m.ns + t] = slab[t]

        for copy in load_g:
            copy.wait()
        total = [jnp.zeros((32, TOK), F32)]

        def use_start(slab):
            total[0] += contract(s["s_all"], m.ns, s["wg"], slab)[0]

        yield from gather(s["s_all"], m.ns, s["s_gather"], s["f_buffers"][4], use_start)
        left = split3(total[0])
        for copy in load_x:
            copy.wait()
        yield from reduce(m.nl, left, s["wx"], s["l_buffers"], s["l_reduce"])

        @pl.when(active)
        def _():
            total = summed_over_y(m.nl, s["l_buffers"], s["l_reduce"])
            for t in range(m.nl):
                s["l_zs"][t] = total[t]

        lz_ss, lz_rs = s["lz_sems"]
        send(
            [(s["l_zs"], s["l_z"].at[z], lz_rs, device(y, (z + k) % NZ, x, c)) for k in FAR],
            lz_ss, s["l_z"].at[pl.ds(0, 7)], active,
        )
        yield

        @pl.when(active)
        def _():
            for t in range(m.nl):
                s["l_z"][z, t] = s["l_zs"][t]
            arrive(s["l_z"].at[pl.ds(0, 7)], lz_rs)
            for t in range(m.nl):
                total = s["l_z"][0, t]
                for zz in range(1, NZ):
                    total = total + s["l_z"][zz, t]
                s["l_all"][x, y * m.nl + t] = total

        side = [jnp.zeros((32, TOK), F32), jnp.zeros((32, 96), F32)]

        def use_left(slab):
            part, pieces = contract(s["l_all"], m.nl, s["wx"], slab)
            side[0] += part
            side[1] += fold3(lax.dot_general(pieces, pieces, NT, preferred_element_type=F32))

        yield from gather(s["l_all"], m.nl, s["l_gather"], s["l_z"], use_left)
        grams[m] = side[1]
        right = split3(side[0])
        yield from reduce(m.ns, right, s["wg"], s["f_buffers"], s["f_reduce"])

        @pl.when(active)
        def _():
            total = summed_over_y(m.ns, s["f_buffers"], s["f_reduce"])
            for zz in range(NZ):
                t, first = divmod(m.lanes * zz, 128)
                if first + m.lanes <= 128:
                    s["f_zs"][zz] = total[t]
                else:
                    s["f_zs"][zz] = jnp.where(lane >= first, total[t], total[t + 1])

        fz_ss, fz_rs = s["fz_sems"]
        send(
            [(s["f_zs"].at[(z + k) % NZ], s["f_z"].at[z], fz_rs, device(y, (z + k) % NZ, x, c)) for k in FAR],
            fz_ss, s["f_z"].at[pl.ds(0, 7)], active,
        )
        yield

        @pl.when(active)
        def _():
            arrive(s["f_z"].at[pl.ds(0, 7)], fz_rs)
            total = s["f_zs"][z]
            for k in range(1, 8):
                total = total + s["f_z"][(z + k) % NZ]
            s["f_own"][...] = total

        last_ss, last_rs = s["last_sems"]
        send(
            [
                (s["f_own"], s["f_last"].at[x], last_rs, device(y, z, (x + k // 2) % NX, (c + k) % 2))
                for k in (4, 5, 2, 3, 6, 7, 1)
            ],
            last_ss, s["f_z"].at[pl.ds(0, 7)], active,
        )

        @pl.when(active)
        def _():
            s["f_last"][x] = s["f_own"][...]

        yield
        arrive(s["f_last"].at[pl.ds(0, 3)], last_rs, active)
        arrive(s["f_last"], last_rs, passive)
        raw = jnp.concatenate([s["f_last"][g] for g in range(GROUPS)], axis=0)
        own = exact_dot(pick, raw, NT)
        out[m.put_factor:m.put_factor + 16, :] = exact_dot(own, inverse[m], NT) * (1.0 / 512)

    def cholesky():
        row, column = iota((32, 32), 0), iota((32, 32), 1)
        rows = iota((32, 1), 0)
        state = {}
        for m in (ENTRY, EXIT):
            gram = grams[m]
            state[m] = [
                gram[:, 0:32] + gram[:, 32:64] + gram[:, 64:96],
                jnp.where(row == column, 1.0, 0.0).astype(F32),
                jnp.ones((32, 1), F32),
            ]
        for j in range(32):
            for m in (ENTRY, EXIT):
                left, unit, diagonal = state[m]
                pivot = left[j:j + 1, j:j + 1]
                factor = jnp.where(rows > j, left[:, j:j + 1] / pivot, 0.0)
                state[m] = [
                    left - factor * left[j:j + 1, :],
                    unit - factor * unit[j:j + 1, :],
                    jnp.where(rows == j, pivot, diagonal),
                ]
            if j == 15:
                yield
        for m, s in ((ENTRY, entry_scratch), (EXIT, exit_scratch)):
            inverse[m] = state[m][1] / jnp.sqrt(state[m][2])
            shape = (8, 128 * m.nl)
            at = m.left_rows * (8 * z + spot)
            pick = jnp.where(
                (iota(shape, 1) == at + iota(shape, 0)) & (iota(shape, 0) < m.left_rows), 1.0, 0.0
            ).astype(F32)
            own = exact_dot(pick, tiles(s["l_all"], y * m.nl, m.nl), NT)
            out[m.put_basis:m.put_basis + 8, :] = exact_dot(own, inverse[m], NT) * math.sqrt(m.width)
        yield

    chains = [
        chain(ENTRY, starts[0], entry_scratch, loads[0:2], loads[4:6]),
        chain(EXIT, starts[1], exit_scratch, loads[2:4], loads[6:8]),
    ]
    for step in chains:
        next(step)
    pl.semaphore_wait(barrier, len(peers))
    extra = None
    while chains:
        issued.append([])
        chains = [step for step in chains if next(step, chains) is None]
        drain(2)
        if extra is None and len(grams) == 2:
            extra = cholesky()
        if extra is not None:
            next(extra, None)
    drain(0)


def outputs_kernel(packed, entry_basis, exit_basis, entry_factor, exit_factor):
    entry_basis[...] = packed[0:6, :]
    exit_basis[...] = packed[8:16, :]
    entry_factor[...] = packed[16:28, :]
    exit_factor[...] = packed[32:38, :]


def scratch_of(m):
    dma = pltpu.SemaphoreType.DMA

    def f32(*shape):
        return pltpu.VMEM(shape + (8, 128), F32)

    def gather_sems():
        return [dma, dma((2,)), dma((2,)), dma((2,)), dma((2,)), dma((2,))]

    def reduce_sems():
        return [dma((2,)), dma((2,)), dma((2,)), dma((2,)), dma, dma]

    def reduce_buffers(n):
        return [f32(4, 8 * n), f32(4, 4 * n), f32(4, 4 * n), f32(4, n), f32(8, n)]

    return {
        "wg": pltpu.VMEM((TOK, m.outs), BF16),
        "wx": pltpu.VMEM((TOK, m.width), BF16),
        "start": pltpu.VMEM((m.right_rows, 32), F32),
        "own": pltpu.VMEM((16, 32), F32),
        "first_send": f32(4), "first_recv": f32(8), "first_sems": [dma((2,)), dma],
        "zs_send": f32(), "zs_recv": f32(8), "zs_sems": [dma, dma],
        "s_all": f32(4, 8 * m.ns), "s_gather": gather_sems(),
        "l_buffers": reduce_buffers(m.nl), "l_reduce": reduce_sems(),
        "l_zs": f32(m.nl), "l_z": f32(8, m.nl), "lz_sems": [dma, dma],
        "l_all": f32(4, 8 * m.nl), "l_gather": gather_sems(),
        "f_buffers": reduce_buffers(m.ns), "f_reduce": reduce_sems(),
        "f_zs": f32(8), "f_z": f32(8), "fz_sems": [dma, dma],
        "f_own": f32(), "f_last": f32(4), "last_sems": [dma, dma],
    }


def body(*args):
    vmem = pl.BlockSpec(memory_space=pltpu.VMEM)
    hbm = pl.BlockSpec(memory_space=pltpu.HBM)
    packed = pl.pallas_call(
        kernel,
        out_shape=jax.ShapeDtypeStruct((48, 32), F32),
        in_specs=[hbm] * 10,
        out_specs=vmem,
        scratch_shapes=[pltpu.SemaphoreType.DMA((10,)), scratch_of(ENTRY), scratch_of(EXIT)],
        compiler_params=pltpu.CompilerParams(
            collective_id=0, has_side_effects=True, vmem_limit_bytes=63 * 1024 * 1024
        ),
        name="powersgd",
    )(*args)
    return pl.pallas_call(
        outputs_kernel,
        out_shape=tuple(jax.ShapeDtypeStruct((rows, 32), F32) for rows in (6, 8, 12, 6)),
        in_specs=[vmem],
        out_specs=(vmem,) * 4,
        name="outputs",
    )(packed)


def solution(mesh):
    spec = P("dp", None)
    return jax.shard_map(body, mesh=mesh, in_specs=(spec,) * 10, out_specs=(spec,) * 4, check_vma=False)
```

```python
import math

import jax
import jax.numpy as jnp
from jax import lax
from jax.experimental import pallas as pl
from jax.experimental.pallas import tpu as pltpu
from jax.sharding import PartitionSpec as P

MESH = pl.DeviceIdType.MESH
NY, NZ, NX = 8, 8, 4
GROUPS = 4
HALF = 4
FAR = (4, 3, 5, 2, 6, 1, 7)
FAR_X = (2, 1, 3)
TOK = 144
F32 = jnp.float32
BF16 = jnp.bfloat16
NT = (((1,), (1,)), ((), ()))
NN = (((1,), (0,)), ((), ()))
TN = (((0,), (0,)), ((), ()))


class Matrix:
    def __init__(self, width, outs, put_basis, put_factor):
        self.width, self.outs = width, outs
        self.nl, self.ns = width // (NY * 128), outs // (NY * 128)
        self.left_rows, self.right_rows = width // 512, outs // 512
        self.lanes = outs // (NY * NZ)
        self.put_basis, self.put_factor = put_basis, put_factor


ENTRY = Matrix(3072, 6144, 0, 16)
EXIT = Matrix(4096, 3072, 8, 32)


def device(y, z, x, c):
    return ((y * NZ + z) * NX + x) * 2 + c


def split3(v):
    hi = v.astype(BF16)
    rest = v - hi.astype(F32)
    mid = rest.astype(BF16)
    lo = (rest - mid.astype(F32)).astype(BF16)
    return jnp.concatenate([hi, mid, lo], axis=0)


def fold3(v):
    return v[0:32] + v[32:64] + v[64:96]


def exact_dot(a, b, dims):
    return lax.dot_general(a, b, dims, precision=lax.Precision.HIGHEST, preferred_element_type=F32)


def iota(shape, dim):
    return lax.broadcasted_iota(jnp.int32, shape, dim)


def kernel(
    entry_input, entry_grad, exit_input, exit_grad,
    entry_left, entry_right, exit_left, exit_right,
    entry_start, exit_start,
    out, load_sem, entry_scratch, exit_scratch,
):
    me = lax.axis_index("dp")
    y, z, x, c = me // (NZ * NX * 2), (me // (NX * 2)) % NZ, (me // 2) % NX, me % 2
    active_core = y // HALF
    active = c == active_core
    passive = c != active_core
    other = device(y, z, x, 1 - c)
    spot = 2 * x + c
    pair = (y // 2) % 2
    issued = [[]]

    def remote(src, dst, ss, rs, target):
        return pltpu.make_async_remote_copy(
            src_ref=src, dst_ref=dst, send_sem=ss, recv_sem=rs, device_id=(target,), device_id_type=MESH
        )

    def guarded(cond, fn):
        if cond is None:
            fn()
        else:
            @pl.when(cond)
            def _():
                fn()

    def send(copies, ss, moved, cond=None):
        def start():
            for src, dst, rs, target in copies:
                remote(src, dst, ss, rs, target).start()

        guarded(cond, start)
        issued[-1].append((cond, remote(moved, moved, ss, ss, other)))

    def arrive(dst, rs, cond=None):
        guarded(cond, remote(dst, dst, rs, rs, other).wait_recv)

    def drain(rounds):
        while len(issued) > rounds:
            for cond, copy in issued.pop(0):
                guarded(cond, copy.wait_send)

    barrier = pltpu.get_barrier_semaphore()
    peers = []
    for k in FAR:
        peers += [device((y + k) % NY, z, x, c), device(y, (z + k) % NZ, x, c)]
    peers += [device(y, z, (x + k // 2) % NX, (c + k) % 2) for k in (4, 5, 2, 3, 6, 7, 1)]
    for peer in peers:
        pl.semaphore_signal(barrier, inc=1, device_id=(peer,), device_id_type=MESH)

    starts = []
    for i, (src, s) in enumerate(((entry_start, entry_scratch), (exit_start, exit_scratch))):
        copy = pltpu.make_async_copy(src, s["start"], load_sem.at[8 + i])
        copy.start()
        starts.append(copy)
    loads = []
    for i, (src, dst, row, rows) in enumerate((
        (entry_grad, entry_scratch["wg"], 0, 128), (entry_right, entry_scratch["wg"], 128, 16),
        (exit_grad, exit_scratch["wg"], 0, 128), (exit_right, exit_scratch["wg"], 128, 16),
        (entry_input, entry_scratch["wx"], 0, 128), (entry_left, entry_scratch["wx"], 128, 16),
        (exit_input, exit_scratch["wx"], 0, 128), (exit_left, exit_scratch["wx"], 128, 16),
    )):
        copy = pltpu.make_async_copy(src, dst.at[pl.ds(row, rows)], load_sem.at[i])
        copy.start()
        loads.append(copy)

    def tiles(whole, first, count):
        return jnp.concatenate(
            [jnp.concatenate([whole[g, first + t] for t in range(count)], axis=1) for g in range(GROUPS)], axis=0
        )

    def columns(ref, slab, count):
        return ref[:, pl.ds(pl.multiple_of(slab * (128 * count), 128), 128 * count)]

    def contract(whole, n, weights, slab):
        pieces = split3(tiles(whole, slab * n, n))
        part = lax.dot_general(pieces, columns(weights, slab, n), NT, preferred_element_type=F32)
        return fold3(part), pieces

    def expand(pieces, weights, slab, n, whole):
        part = fold3(lax.dot_general(pieces, columns(weights, slab, n), NN, preferred_element_type=F32))
        for g in range(GROUPS):
            for t in range(n):
                whole[g, slab * n + t] = part[8 * g:8 * g + 8, 128 * t:128 * t + 128]

    def batches(half, far_first):
        near = jnp.where(half == active_core, pair, 1 - pair)
        first = 1 - near if far_first else near
        return [(b, HALF * half + 2 * b) for b in (first, 1 - first)]

    def gather(whole, n, sems, moved, use):
        ys, yr, xs, xr, cs, cr = sems

        def part(group, slab, count):
            return whole.at[group, pl.ds(slab * n, count * n)]

        def full(slab):
            return whole.at[:, pl.ds(slab * n, 2 * n)]

        mine = part(x, y, 1)
        send(
            [(mine, mine, yr.at[(y // 2) % 2], device((y + k) % NY, z, x, c)) for k in FAR],
            ys, moved.at[pl.ds(0, 7)], active,
        )
        yield
        for b, slab in batches(c, False):
            own = active & (b == pair)
            arrive(part(x, slab, 1), yr.at[b], own)
            arrive(part(x, slab, 2), yr.at[b], jnp.logical_not(own))
            both = part(x, slab, 2)
            send(
                [(both, both, xr.at[b], device(y, z, (x + k) % NX, c)) for k in FAR_X],
                xs.at[b], whole.at[pl.ds(0, 3), pl.ds(0, 2 * n)],
            )
        yield
        for b, slab in batches(c, False):
            arrive(whole.at[pl.ds(0, 3), pl.ds(0, 2 * n)], xr.at[b])
            send([(full(slab), full(slab), cr.at[b], other)], cs.at[b], full(slab))
            use(slab)
            use(slab + 1)
        for b, slab in batches(1 - c, False):
            arrive(full(slab), cr.at[b])
            use(slab)
            use(slab + 1)

    def reduce(n, pieces, weights, buffers, sems):
        local, from_core, from_x, y_send, from_y = buffers
        cs, cr, xs, xr, ys, yr = sems
        def give(b, slab):
            expand(pieces, weights, slab, n, local)
            expand(pieces, weights, slab + 1, n, local)
            src = local.at[:, pl.ds(slab * n, 2 * n)]
            send([(src, from_core.at[:, pl.ds(2 * b * n, 2 * n)], cr.at[b], other)], cs.at[b], src)

        theirs, ours = batches(1 - c, True), batches(c, True)
        give(*theirs[0])
        for i, (b, slab) in enumerate(ours):
            expand(pieces, weights, slab, n, local)
            expand(pieces, weights, slab + 1, n, local)
            if i == 0:
                give(*theirs[1])
            arrive(from_core.at[:, pl.ds(2 * b * n, 2 * n)], cr.at[b])
            for g in range(GROUPS):
                for t in range(2 * n):
                    local[g, slab * n + t] = local[g, slab * n + t] + from_core[g, 2 * b * n + t]
            send(
                [
                    (
                        local.at[(x + k) % NX, pl.ds(slab * n, 2 * n)], from_x.at[x, pl.ds(2 * b * n, 2 * n)],
                        xr.at[b], device(y, z, (x + k) % NX, c),
                    )
                    for k in FAR_X
                ],
                xs.at[b], from_x.at[pl.ds(0, 3), pl.ds(0, 2 * n)],
            )
        yield
        for b, slab in batches(c, True):
            arrive(from_x.at[pl.ds(0, 3), pl.ds(0, 2 * n)], xr.at[b])
            for i in range(2):
                for t in range(n):
                    total = local[x, (slab + i) * n + t]
                    for k in range(1, 4):
                        total = total + from_x[(x + k) % NX, (2 * b + i) * n + t]
                    y_send[2 * b + i, t] = total
                copy = remote(
                    y_send.at[2 * b + i], from_y.at[y], ys, yr, device(slab + i, z, x, c)
                )
                guarded(slab + i != y, copy.start)
        issued[-1].append((active, remote(from_y.at[pl.ds(0, 3)], from_y.at[pl.ds(0, 3)], ys, ys, other)))
        issued[-1].append((passive, remote(from_y.at[pl.ds(0, 4)], from_y.at[pl.ds(0, 4)], ys, ys, other)))
        yield

    def summed_over_y(n, buffers, sems):
        y_send, from_y = buffers[3:]
        arrive(from_y.at[pl.ds(0, 7)], sems[5])
        total = [y_send[y % HALF, t] for t in range(n)]
        for k in range(1, 8):
            for t in range(n):
                total[t] = total[t] + from_y[(y + k) % NY, t]
        return total

    lane = iota((8, 128), 1)
    grams, inverse = {}, {}

    def chain(m, start, s, load_g, load_x):
        rows = m.right_rows
        s["own"][...] = jnp.zeros_like(s["own"])
        start.wait()
        s["own"][0:rows, :] = s["start"][...]
        at = m.lanes * z + rows * spot
        pick = jnp.where(
            (iota((16, 128), 1) == (at + iota((16, 128), 0)) % 128) & (iota((16, 128), 0) < rows), 1.0, 0.0
        ).astype(F32)
        placed = exact_dot(s["own"][...], pick, TN)
        for g in range(GROUPS):
            s["first_send"][g] = placed[8 * g:8 * g + 8, :]
        yield
        first_ss, first_rs = s["first_sems"]
        landing = s["first_recv"].at[spot]
        send([(s["first_send"].at[x], landing, first_rs, other)], first_ss.at[0], s["first_send"].at[0], passive)
        send(
            [
                (s["first_send"].at[(x + k) % NX], landing, first_rs, device(y, z, (x + k) % NX, active_core))
                for k in FAR_X
            ],
            first_ss.at[1], s["first_send"].at[pl.ds(0, 3)],
        )
        yield

        @pl.when(active)
        def _():
            arrive(s["first_recv"].at[pl.ds(0, 7)], first_rs)
            total = s["first_send"][x]
            for k in range(1, 8):
                total = total + s["first_recv"][(spot + k) % 8]
            s["zs_send"][...] = total

        zs_ss, zs_rs = s["zs_sems"]
        send(
            [(s["zs_send"], s["zs_recv"].at[z], zs_rs, device(y, (z + k) % NZ, x, c)) for k in FAR],
            zs_ss, s["zs_recv"].at[pl.ds(0, 7)], active,
        )
        yield

        @pl.when(active)
        def _():
            s["zs_recv"][z] = s["zs_send"][...]
            arrive(s["zs_recv"].at[pl.ds(0, 7)], zs_rs)
            slab = [jnp.zeros((8, 128), F32) for _ in range(m.ns)]
            for zz in range(NZ):
                t, first = divmod(m.lanes * zz, 128)
                piece = s["zs_recv"][zz]
                if first + m.lanes <= 128:
                    slab[t] = slab[t] + piece
                else:
                    slab[t] = slab[t] + jnp.where(lane >= first, piece, 0.0)
                    slab[t + 1] = slab[t + 1] + jnp.where(lane < first, piece, 0.0)
            for t in range(m.ns):
                s["s_all"][x, y * m.ns + t] = slab[t]

        for copy in load_g:
            copy.wait()
        total = [jnp.zeros((32, TOK), F32)]

        def use_start(slab):
            total[0] += contract(s["s_all"], m.ns, s["wg"], slab)[0]

        yield from gather(s["s_all"], m.ns, s["s_gather"], s["f_buffers"][4], use_start)
        left = split3(total[0])
        for copy in load_x:
            copy.wait()
        yield from reduce(m.nl, left, s["wx"], s["l_buffers"], s["l_reduce"])

        @pl.when(active)
        def _():
            total = summed_over_y(m.nl, s["l_buffers"], s["l_reduce"])
            for t in range(m.nl):
                s["l_zs"][t] = total[t]

        lz_ss, lz_rs = s["lz_sems"]
        send(
            [(s["l_zs"], s["l_z"].at[z], lz_rs, device(y, (z + k) % NZ, x, c)) for k in FAR],
            lz_ss, s["l_z"].at[pl.ds(0, 7)], active,
        )
        yield

        @pl.when(active)
        def _():
            for t in range(m.nl):
                s["l_z"][z, t] = s["l_zs"][t]
            arrive(s["l_z"].at[pl.ds(0, 7)], lz_rs)
            for t in range(m.nl):
                total = s["l_z"][0, t]
                for zz in range(1, NZ):
                    total = total + s["l_z"][zz, t]
                s["l_all"][x, y * m.nl + t] = total

        side = [jnp.zeros((32, TOK), F32), jnp.zeros((32, 96), F32)]

        def use_left(slab):
            part, pieces = contract(s["l_all"], m.nl, s["wx"], slab)
            side[0] += part
            side[1] += fold3(lax.dot_general(pieces, pieces, NT, preferred_element_type=F32))

        yield from gather(s["l_all"], m.nl, s["l_gather"], s["l_z"], use_left)
        grams[m] = side[1]
        right = split3(side[0])
        yield from reduce(m.ns, right, s["wg"], s["f_buffers"], s["f_reduce"])

        @pl.when(active)
        def _():
            total = summed_over_y(m.ns, s["f_buffers"], s["f_reduce"])
            for zz in range(NZ):
                t, first = divmod(m.lanes * zz, 128)
                if first + m.lanes <= 128:
                    s["f_zs"][zz] = total[t]
                else:
                    s["f_zs"][zz] = jnp.where(lane >= first, total[t], total[t + 1])

        fz_ss, fz_rs = s["fz_sems"]
        send(
            [(s["f_zs"].at[(z + k) % NZ], s["f_z"].at[z], fz_rs, device(y, (z + k) % NZ, x, c)) for k in FAR],
            fz_ss, s["f_z"].at[pl.ds(0, 7)], active,
        )
        yield

        @pl.when(active)
        def _():
            arrive(s["f_z"].at[pl.ds(0, 7)], fz_rs)
            total = s["f_zs"][z]
            for k in range(1, 8):
                total = total + s["f_z"][(z + k) % NZ]
            s["f_own"][...] = total

        last_ss, last_rs = s["last_sems"]
        send(
            [
                (s["f_own"], s["f_last"].at[x], last_rs, device(y, z, (x + k // 2) % NX, (c + k) % 2))
                for k in (4, 5, 2, 3, 6, 7, 1)
            ],
            last_ss, s["f_z"].at[pl.ds(0, 7)], active,
        )

        @pl.when(active)
        def _():
            s["f_last"][x] = s["f_own"][...]

        yield
        arrive(s["f_last"].at[pl.ds(0, 3)], last_rs, active)
        arrive(s["f_last"], last_rs, passive)
        raw = jnp.concatenate([s["f_last"][g] for g in range(GROUPS)], axis=0)
        own = exact_dot(pick, raw, NT)
        out[m.put_factor:m.put_factor + 16, :] = exact_dot(own, inverse[m], NT) * (1.0 / 512)

    def cholesky():
        row, column = iota((32, 32), 0), iota((32, 32), 1)
        rows = iota((32, 1), 0)
        state = {}
        for m in (ENTRY, EXIT):
            gram = grams[m]
            state[m] = [
                gram[:, 0:32] + gram[:, 32:64] + gram[:, 64:96],
                jnp.where(row == column, 1.0, 0.0).astype(F32),
                jnp.ones((32, 1), F32),
            ]
        for j in range(32):
            for m in (ENTRY, EXIT):
                left, unit, diagonal = state[m]
                pivot = left[j:j + 1, j:j + 1]
                factor = jnp.where(rows > j, left[:, j:j + 1] / pivot, 0.0)
                state[m] = [
                    left - factor * left[j:j + 1, :],
                    unit - factor * unit[j:j + 1, :],
                    jnp.where(rows == j, pivot, diagonal),
                ]
            if j == 15:
                yield
        for m, s in ((ENTRY, entry_scratch), (EXIT, exit_scratch)):
            inverse[m] = state[m][1] / jnp.sqrt(state[m][2])
            shape = (8, 128 * m.nl)
            at = m.left_rows * (8 * z + spot)
            pick = jnp.where(
                (iota(shape, 1) == at + iota(shape, 0)) & (iota(shape, 0) < m.left_rows), 1.0, 0.0
            ).astype(F32)
            own = exact_dot(pick, tiles(s["l_all"], y * m.nl, m.nl), NT)
            out[m.put_basis:m.put_basis + 8, :] = exact_dot(own, inverse[m], NT) * math.sqrt(m.width)
        yield

    chains = [
        chain(ENTRY, starts[0], entry_scratch, loads[0:2], loads[4:6]),
        chain(EXIT, starts[1], exit_scratch, loads[2:4], loads[6:8]),
    ]
    for step in chains:
        next(step)
    pl.semaphore_wait(barrier, len(peers))
    extra = None
    while chains:
        issued.append([])
        chains = [step for step in chains if next(step, chains) is None]
        drain(2)
        if extra is None and len(grams) == 2:
            extra = cholesky()
        if extra is not None:
            next(extra, None)
    drain(0)


def outputs_kernel(packed, entry_basis, exit_basis, entry_factor, exit_factor):
    entry_basis[...] = packed[0:6, :]
    exit_basis[...] = packed[8:16, :]
    entry_factor[...] = packed[16:28, :]
    exit_factor[...] = packed[32:38, :]


def scratch_of(m):
    dma = pltpu.SemaphoreType.DMA

    def f32(*shape):
        return pltpu.VMEM(shape + (8, 128), F32)

    def gather_sems():
        return [dma, dma((2,)), dma((2,)), dma((2,)), dma((2,)), dma((2,))]

    def reduce_sems():
        return [dma((2,)), dma((2,)), dma((2,)), dma((2,)), dma, dma]

    def reduce_buffers(n):
        return [f32(4, 8 * n), f32(4, 4 * n), f32(4, 4 * n), f32(4, n), f32(8, n)]

    return {
        "wg": pltpu.VMEM((TOK, m.outs), BF16),
        "wx": pltpu.VMEM((TOK, m.width), BF16),
        "start": pltpu.VMEM((m.right_rows, 32), F32),
        "own": pltpu.VMEM((16, 32), F32),
        "first_send": f32(4), "first_recv": f32(8), "first_sems": [dma((2,)), dma],
        "zs_send": f32(), "zs_recv": f32(8), "zs_sems": [dma, dma],
        "s_all": f32(4, 8 * m.ns), "s_gather": gather_sems(),
        "l_buffers": reduce_buffers(m.nl), "l_reduce": reduce_sems(),
        "l_zs": f32(m.nl), "l_z": f32(8, m.nl), "lz_sems": [dma, dma],
        "l_all": f32(4, 8 * m.nl), "l_gather": gather_sems(),
        "f_buffers": reduce_buffers(m.ns), "f_reduce": reduce_sems(),
        "f_zs": f32(8), "f_z": f32(8), "fz_sems": [dma, dma],
        "f_own": f32(), "f_last": f32(4), "last_sems": [dma, dma],
    }


def body(*args):
    vmem = pl.BlockSpec(memory_space=pltpu.VMEM)
    hbm = pl.BlockSpec(memory_space=pltpu.HBM)
    packed = pl.pallas_call(
        kernel,
        out_shape=jax.ShapeDtypeStruct((48, 32), F32),
        in_specs=[hbm] * 10,
        out_specs=vmem,
        scratch_shapes=[pltpu.SemaphoreType.DMA((10,)), scratch_of(ENTRY), scratch_of(EXIT)],
        compiler_params=pltpu.CompilerParams(
            collective_id=0, has_side_effects=True, vmem_limit_bytes=63 * 1024 * 1024
        ),
        name="powersgd",
    )(*args)
    return pl.pallas_call(
        outputs_kernel,
        out_shape=tuple(jax.ShapeDtypeStruct((rows, 32), F32) for rows in (6, 8, 12, 6)),
        in_specs=[vmem],
        out_specs=(vmem,) * 4,
        name="outputs",
    )(packed)


def solution(mesh):
    spec = P("dp", None)
    return jax.shard_map(body, mesh=mesh, in_specs=(spec,) * 10, out_specs=(spec,) * 4, check_vma=False)
```
